32 devices in a mesh: blocks: 2 (over x), rows: 8 (over z, y), pairs: 2 (over core).
Axes of the slice: x: 2, y: 2, z: 4, core: 2. Of those that a mesh axis runs over, the one named last changes fastest.
Arguments:
- interferograms: bfloat16 [2, 1500, 256, 256], P(None, 'pairs', ('blocks', 'rows')), parts along dimension 2, may hold values from -6 to 6
- pair_dates: int32 [1500, 2], replicated, may hold values from 0 to 299, as said below
- mask_table: int32 [4, 1500], replicated, may hold values 0 or 1
- gap_dates: int32 [4, 30], replicated, may hold values from 0 to 299, as said below
- pattern_ids: int32 [256, 256], P(('blocks', 'rows')), parts along dimension 0, may hold values from 0 to 3
Outputs:
- corrected: float32 [256, 300, 256], P(('blocks', 'rows', 'pairs')), parts along dimension 0
The draws below stay inside these ranges and needn't reach their ends.
There are 2 independent parts, one for each index of `blocks`. The reference program is written for one: setup_inputs(seed, part) draws one part's arguments, and reference() takes and returns one part's arrays. A program takes and returns all parts, laid end to end along the dimension named above; an argument that names none is the same for every part. Nothing has to cross between parts.
Inputs may be any that keep to these rules, and one draw needn't show every extreme that they name: `pair_dates`: row k holds the earlier and the later date of pair k; the later exceeds the earlier by 1 to 5. `gap_dates`: each row lists 30 different dates. `pattern_ids`: each pixel belongs to one of 4 gap pattern classes.
All inputs are finite; a program needn't handle non-finite values.
Results may differ from the reference program's by a relative error of at most 0.0044.
Values may be sent and summed in bfloat16 or wider, within the bound.
A program may use at most 192 MiB of HBM per device.

```python
import jax
import jax.numpy as jnp
from jax import lax

PAIRS = 1500
DATES = 300
NPAT = 4
GAPS = 30
SPAN = 5
RADIUS = 6
ROWS_DEV = 16
COLS = 256
HEIGHT = 128


def draw_pair_dates(key, part):
    key_early, key_span = jax.random.split(key)
    early = jax.random.randint(key_early, (PAIRS,), 0, DATES - 1)
    span = jax.random.randint(key_span, (PAIRS,), 1, SPAN + 1)
    late = jnp.minimum(early + span, DATES - 1)
    index = jnp.arange(PAIRS)
    early = jnp.where(index == 0, 0, early)
    late = jnp.where(index == 0, span, late)
    early = jnp.where(index == 1, DATES - 1 - span, early)
    late = jnp.where(index == 1, DATES - 1, late)
    return jnp.stack([early, late], axis=1).astype(jnp.int32)


def draw_gap_dates(key, part):
    keys = jax.random.split(jax.random.fold_in(key, 11), NPAT)
    shuffled = jax.vmap(lambda one_key: jax.random.permutation(one_key, DATES))(keys)[:, :GAPS]
    inner = jax.random.permutation(jax.random.fold_in(key, 7), DATES - 2)[:GAPS - 2] + 1
    first_row = jnp.concatenate([jnp.array([0, DATES - 1]), inner])
    return shuffled.at[0].set(first_row).astype(jnp.int32)


def set_ends(values, key, least, high):
    longest = values.shape.index(max(values.shape))
    spots = []
    for shift in (0, 1):
        where = [jax.random.randint(jax.random.fold_in(key, axis), (), 0, length) for axis, length in enumerate(values.shape)]
        where[longest] = (where[longest] + shift) % values.shape[longest]
        spots.append(tuple(where))
    return values.at[spots[0]].set(least).at[spots[1]].set(high)


def block_levels(own_key, extent, cuts, smallest, high):
    loudness = 1.0
    for dim, blocks in cuts:
        steps = jax.random.uniform(jax.random.fold_in(jax.random.fold_in(own_key, 6), dim), (blocks,), jnp.float32, smallest / len(cuts), high / len(cuts))
        loudness = loudness * jnp.repeat(jnp.exp(steps), extent[dim] // blocks).reshape((-1,) + (1,) * (len(extent) - 1 - dim))
    return loudness


def noise(own_key, dims, spread, most, pieces=(), held_as=jnp.bfloat16):
    values = spread * jax.random.normal(own_key, dims, jnp.float32)
    if pieces:
        values = values * block_levels(own_key, dims, pieces, -0.22, 0.18)
    return jnp.clip(values, -most, most).astype(held_as)


def setup_inputs(seed: int = 0, part: int = 0) -> dict:
    key_of = jax.random.split(jax.random.key(seed), 6)
    own_keys = jax.random.split(jax.random.fold_in(key_of[5], part), 6)
    interferograms = noise(own_keys[0], (2, PAIRS, HEIGHT, COLS), 1.0, 6.0, ((1, 2), (2, 8)))
    pair_dates = draw_pair_dates(jax.random.fold_in(key_of[5], 71), part)
    mask_table = set_ends((jax.random.randint(key_of[2], (NPAT, PAIRS), 0, 5) < 4).astype(jnp.int32), jax.random.fold_in(key_of[2], 1), 0, 1)
    gap_dates = draw_gap_dates(jax.random.fold_in(key_of[5], 71), part)
    pattern_ids = set_ends(jax.random.randint(own_keys[4], (HEIGHT, COLS), 0, NPAT), jax.random.fold_in(own_keys[4], 1), 0, NPAT - 1).astype(jnp.int32)
    return dict(interferograms=interferograms, pair_dates=pair_dates, mask_table=mask_table, gap_dates=gap_dates, pattern_ids=pattern_ids)


damping = 0.5
corr_length = 10.0
gauss_width = 2.0

def build_operators(pair_dates, mask_rows, gap_rows):
    dates = jnp.arange(DATES, dtype=jnp.int32)
    first_hot = (dates[None, :] == pair_dates[:, 0:1]).astype(jnp.float32)
    second_hot = (dates[None, :] == pair_dates[:, 1:2]).astype(jnp.float32)
    incidence = second_hot - first_hot
    gapped = jnp.any(gap_rows[:, :, None] == dates[None, None, :], axis=1).astype(jnp.float32)
    lag = jnp.abs(dates[:, None] - dates[None, :]).astype(jnp.float32)
    cov = jnp.exp(-lag / corr_length)
    ident = jnp.eye(DATES, dtype=jnp.float32)
    hp = lax.Precision.HIGHEST

    def single(args):
        valid_row, gap_row = args
        gap_first = jnp.dot(first_hot, gap_row, precision=hp)
        gap_second = jnp.dot(second_hot, gap_row, precision=hp)
        keep = valid_row.astype(jnp.float32) * (1.0 - gap_first) * (1.0 - gap_second)
        weighted = incidence * keep[:, None]
        normal = jnp.dot(weighted.T, incidence, precision=hp) + damping * ident
        factor = jnp.linalg.cholesky(normal)
        solved = jax.scipy.linalg.cho_solve((factor, True), weighted.T)
        observed = 1.0 - gap_row
        masked = cov * observed[:, None] * observed[None, :] + jnp.diag(gap_row)
        cross = cov * observed[:, None] * gap_row[None, :]
        factor_two = jnp.linalg.cholesky(masked)
        weights = jax.scipy.linalg.cho_solve((factor_two, True), cross)
        return solved + jnp.dot(weights.T, solved, precision=hp)
    return lax.map(single, (mask_rows, gapped)).astype(jnp.bfloat16)

def multilook_one(pair_planes):
    height = pair_planes.shape[1]
    width = pair_planes.shape[2]
    planes = pair_planes.astype(jnp.float32)
    padded = jnp.pad(planes, ((0, 0), (2, 2), (2, 2)))
    along = sum((padded[:, offset:offset + height, :] for offset in range(5)))
    boxed = sum((along[:, :, offset:offset + width] for offset in range(5)))
    modulus = jnp.sqrt(boxed[0] * boxed[0] + boxed[1] * boxed[1])
    return (boxed[1] / jnp.maximum(modulus, 1.0)).astype(jnp.bfloat16)

def gauss_kernel():
    spots = jnp.arange(-RADIUS, RADIUS + 1, dtype=jnp.float32)
    raw = jnp.exp(-spots * spots / (2.0 * gauss_width * gauss_width))
    return raw / jnp.sum(raw)

def select_class(by_class, classes_here):
    labels = jnp.arange(by_class.shape[1], dtype=jnp.int32)
    hit = classes_here[:, None, None, :] == labels[None, :, None, None]
    return lax.optimization_barrier(jnp.sum(jnp.where(hit, by_class, 0.0), axis=1))

def reference(interferograms, pair_dates, mask_table, gap_dates, pattern_ids):
    height = interferograms.shape[2]
    width = interferograms.shape[3]
    looks = lax.map(multilook_one, jnp.moveaxis(interferograms, 1, 0))
    operators = build_operators(pair_dates, mask_table, gap_dates).astype(jnp.float32)
    block_rows = ROWS_DEV // 2

    def invert(start):
        piece = lax.dynamic_slice_in_dim(looks, start, block_rows, 1).astype(jnp.float32)
        classes_here = lax.dynamic_slice_in_dim(pattern_ids, start, block_rows, 0)
        by_class = jnp.einsum('qtk,krc->rqtc', operators, piece, precision=lax.Precision.HIGHEST)
        return select_class(by_class, classes_here)
    starts = jnp.arange(height // block_rows, dtype=jnp.int32) * block_rows
    series = lax.map(invert, starts).reshape(height, DATES, width)
    kernel = gauss_kernel()
    padded = jnp.pad(series, ((RADIUS, RADIUS), (0, 0), (RADIUS, RADIUS)))
    along = sum((kernel[offset] * padded[offset:offset + height] for offset in range(2 * RADIUS + 1)))
    screen = sum((kernel[offset] * along[:, :, offset:offset + width] for offset in range(2 * RADIUS + 1)))
    return series - screen
```

```python
import functools

import jax
import ml_dtypes
import numpy as np
import jax.numpy as jnp
from jax import lax
from jax.experimental import pallas as pl
from jax.experimental.pallas import tpu as pltpu
from jax.sharding import PartitionSpec as P

DATES = 300
NPAT = 4
SPAN = 5
RADIUS = 6
LANES = 128
BLOCKS = DATES // SPAN
BLOCKS_PAD = 64
DATES_PAD = 304
LEVELS = 6
RIM = 32


damping = 0.5
corr_length = 10.0
gauss_width = 2.0


def round_up(value, unit):
    return -(-value // unit) * unit


def block_matmul(left, right, transposed=False):
    size = len(left)
    out = []
    for a in range(size):
        row = []
        for b in range(size):
            total = None
            for m in range(size):
                term = left[a][m] * (right[b][m] if transposed else right[m][b])
                total = term if total is None else total + term
            row.append(total)
        out.append(row)
    return out


def block_inverse(matrix):
    size = len(matrix)
    work = [list(row) for row in matrix]
    for k in range(size):
        pivot = 1.0 / work[k][k]
        work[k] = [pivot if j == k else work[k][j] * pivot for j in range(size)]
        for i in range(size):
            if i != k:
                factor = work[i][k]
                work[i] = [
                    -factor * pivot if j == k else work[i][j] - factor * work[k][j]
                    for j in range(size)
                ]
    return work


def moved(blocks, shift):
    return [[pltpu.roll(item, shift % LANES, 1) for item in row] for row in blocks]


def reduction_kernel(keep_ref, early_ref, late_ref, coef_ref):
    early = early_ref[...]
    span = late_ref[...] - early
    keep = keep_ref[...]
    classes = keep.shape[0]
    picked = jnp.concatenate(
        [jnp.where(span == d, keep, 0.0) for d in range(1, SPAN + 1)], axis=0
    ).astype(jnp.bfloat16)
    count = {}
    for a in range(SPAN):
        date = SPAN * lax.broadcasted_iota(jnp.int32, (LANES, early.shape[1]), 0) + a
        hot = jnp.where(date == early, 1.0, 0.0).astype(jnp.bfloat16)
        counts = lax.dot_general(
            picked, hot, (((1,), (1,)), ((), ())), preferred_element_type=jnp.float32
        )
        for d in range(1, SPAN + 1):
            count[d, a] = counts[(d - 1) * classes : d * classes]
    diagonal, upper = [], []
    for a in range(SPAN):
        total = damping
        for d in range(1, SPAN + 1):
            total = total + count[d, a]
            if a >= d:
                total = total + count[d, a - d]
            else:
                total = total + pltpu.roll(count[d, a - d + SPAN], 1, 1)
        diagonal.append(
            [total if b == a else -count[abs(b - a), min(a, b)] for b in range(SPAN)]
        )
        zero = jnp.zeros_like(total)
        upper.append([-count[SPAN + b - a, a] if b <= a else zero for b in range(SPAN)])
    slot = 0
    step = 1
    while step < BLOCKS:
        inverse = block_inverse(diagonal)
        flipped = [list(row) for row in zip(*upper)]
        below = block_matmul(flipped, inverse)
        gamma = [[-x for x in row] for row in block_matmul(upper, moved(inverse, -step))]
        alpha = [[-x for x in row] for row in moved(below, step)]
        first = moved(block_matmul(below, upper), step)
        second = block_matmul(gamma, upper, transposed=True)
        diagonal = [
            [diagonal[a][b] - first[a][b] + second[a][b] for b in range(SPAN)]
            for a in range(SPAN)
        ]
        upper = block_matmul(gamma, moved(upper, -step))
        for part in (alpha, gamma):
            for row in part:
                for item in row:
                    coef_ref[slot] = item
                    slot += 1
        step *= 2
    for row in block_inverse(diagonal):
        for item in row:
            coef_ref[slot] = item
            slot += 1


def inverse_kernel(coef_ref, mix_ref, high_ref, mid_ref, low_ref, state_ref, flat_ref):
    tile = pl.program_id(1)
    state_ref[...] = jnp.zeros_like(state_ref)
    column = lax.broadcasted_iota(jnp.int32, (BLOCKS_PAD, LANES), 1) + tile * LANES
    date = SPAN * lax.broadcasted_iota(jnp.int32, (BLOCKS_PAD, LANES), 0)
    for a in range(SPAN):
        state_ref[a, RIM : RIM + BLOCKS_PAD] = jnp.where(date + a == column, 1.0, 0.0)
    coef = coef_ref[0]
    slot = 0
    step = 1
    while step < BLOCKS:
        before = [state_ref[b, RIM - step : RIM - step + BLOCKS_PAD] for b in range(SPAN)]
        after = [state_ref[b, RIM + step : RIM + step + BLOCKS_PAD] for b in range(SPAN)]
        fresh = [state_ref[a, RIM : RIM + BLOCKS_PAD] for a in range(SPAN)]
        for part in (before, after):
            for a in range(SPAN):
                for b in range(SPAN):
                    fresh[a] = fresh[a] + coef[:, slot : slot + 1] * part[b]
                    slot += 1
        for a in range(SPAN):
            state_ref[a, RIM : RIM + BLOCKS_PAD] = fresh[a]
        step *= 2
    last = [state_ref[b, RIM : RIM + BLOCKS_PAD] for b in range(SPAN)]
    for a in range(SPAN):
        total = None
        for b in range(SPAN):
            term = coef[:, slot : slot + 1] * last[b]
            total = term if total is None else total + term
            slot += 1
        flat_ref[a * BLOCKS_PAD : (a + 1) * BLOCKS_PAD] = total
    mixed = jnp.dot(
        mix_ref[0],
        flat_ref[...],
        precision=lax.Precision.HIGHEST,
        preferred_element_type=jnp.float32,
    )
    high = mixed.astype(jnp.bfloat16)
    rest = mixed - high.astype(jnp.float32)
    mid = rest.astype(jnp.bfloat16)
    high_ref[0] = high
    mid_ref[0] = mid
    low_ref[0] = (rest - mid.astype(jnp.float32)).astype(jnp.bfloat16)


def operator_kernel(high_ref, mid_ref, low_ref, early_ref, late_ref, keep_ref, out_ref):
    date = lax.broadcasted_iota(jnp.int32, (high_ref.shape[2], early_ref.shape[1]), 0)
    plus = jnp.where(date == late_ref[...], 1.0, 0.0)
    minus = jnp.where(date == early_ref[...], 1.0, 0.0)
    incidence = (plus - minus).astype(jnp.bfloat16)
    total = jnp.dot(low_ref[0], incidence, preferred_element_type=jnp.float32)
    total += jnp.dot(mid_ref[0], incidence, preferred_element_type=jnp.float32)
    total += jnp.dot(high_ref[0], incidence, preferred_element_type=jnp.float32)
    out_ref[0] = (total * keep_ref[0]).astype(jnp.bfloat16)


def mixing_matrix(gap_dates):
    classes = gap_dates.shape[0]
    dates = jnp.arange(DATES, dtype=jnp.int32)
    gapped = jnp.any(gap_dates[:, :, None] == dates[None, None, :], axis=1)
    earlier = jnp.where(~gapped[:, None, :] & (dates[None, :] < dates[:, None]), dates, -1)
    later = jnp.where(~gapped[:, None, :] & (dates[None, :] > dates[:, None]), dates, DATES)
    left = jnp.max(earlier, axis=2)
    right = jnp.min(later, axis=2)
    ahead = (right - dates).astype(jnp.float32) / corr_length
    behind = (dates - left).astype(jnp.float32) / corr_length
    whole = jnp.sinh(ahead + behind)
    no_left = left < 0
    no_right = right >= DATES
    from_left = jnp.where(no_right, jnp.exp(-behind), jnp.sinh(ahead) / whole)
    from_right = jnp.where(no_left, jnp.exp(-ahead), jnp.sinh(behind) / whole)
    from_left = jnp.where(gapped & ~no_left, from_left, 0.0)
    from_right = jnp.where(gapped & ~no_right, from_right, 0.0)
    place = jnp.arange(SPAN * BLOCKS_PAD, dtype=jnp.int32)
    source = SPAN * (place % BLOCKS_PAD) + place // BLOCKS_PAD
    source = jnp.where(source < DATES, source, -2)
    mix = jnp.where(source == dates[:, None], 1.0, 0.0)[None]
    mix = mix + jnp.where(source == left[:, :, None], from_left[:, :, None], 0.0)
    mix = mix + jnp.where(source == right[:, :, None], from_right[:, :, None], 0.0)
    return jnp.pad(mix, ((0, 0), (0, DATES_PAD - DATES), (0, 0)))


def build_operators(pair_dates, mask_table, gap_dates, own, width):
    classes, pairs = mask_table.shape
    early, late = pair_dates[:, 0], pair_dates[:, 1]
    lost = jnp.any(
        (gap_dates[:, :, None] == early) | (gap_dates[:, :, None] == late), axis=1
    )
    keep = jnp.where(lost, 0.0, mask_table.astype(jnp.float32))
    padded = round_up(pairs, LANES)
    keep_all = jnp.pad(keep, ((0, round_up(classes, 8) - classes), (0, padded - pairs)))
    early_all = jnp.pad(early[None], ((0, 0), (0, padded - pairs)), constant_values=-1)
    late_all = jnp.pad(late[None], ((0, 0), (0, padded - pairs)), constant_values=-1)
    slots = (2 * LEVELS + 1) * SPAN * SPAN
    coef = pl.pallas_call(
        reduction_kernel,
        out_shape=jax.ShapeDtypeStruct((slots, keep_all.shape[0], LANES), jnp.float32),
        compiler_params=pltpu.CompilerParams(vmem_limit_bytes=48 << 20),
    )(keep_all, early_all, late_all)
    coef = jnp.transpose(coef[:, :classes, :BLOCKS_PAD], (1, 2, 0))
    mix = mixing_matrix(gap_dates)
    wide = round_up(DATES, LANES)
    piece = pl.BlockSpec((1, DATES_PAD, LANES), lambda q, j: (q, 0, j))
    shape = jax.ShapeDtypeStruct((classes, DATES_PAD, wide), jnp.bfloat16)
    parts = pl.pallas_call(
        inverse_kernel,
        grid=(classes, wide // LANES),
        in_specs=[
            pl.BlockSpec((1, BLOCKS_PAD, slots), lambda q, j: (q, 0, 0)),
            pl.BlockSpec((1, DATES_PAD, SPAN * BLOCKS_PAD), lambda q, j: (q, 0, 0)),
        ],
        out_specs=[piece] * 3,
        out_shape=[shape] * 3,
        scratch_shapes=[
            pltpu.VMEM((SPAN, BLOCKS_PAD + 2 * RIM, LANES), jnp.float32),
            pltpu.VMEM((SPAN * BLOCKS_PAD, LANES), jnp.float32),
        ],
        compiler_params=pltpu.CompilerParams(vmem_limit_bytes=48 << 20),
    )(coef, mix)
    count = pairs // own[1]
    begin = own[0] * count
    cut = lambda value, fill: jnp.pad(
        lax.dynamic_slice_in_dim(value, begin, count, 1),
        ((0, 0), (0, width - count)),
        constant_values=fill,
    )
    full = pl.BlockSpec((1, DATES_PAD, wide), lambda q: (q, 0, 0))
    line = pl.BlockSpec((1, width), lambda q: (0, 0))
    return pl.pallas_call(
        operator_kernel,
        grid=(classes,),
        in_specs=[full] * 3 + [line] * 2 + [pl.BlockSpec((1, 1, width), lambda q: (q, 0, 0))],
        out_specs=pl.BlockSpec((1, DATES_PAD, width), lambda q: (q, 0, 0)),
        out_shape=jax.ShapeDtypeStruct((classes, DATES_PAD, width), jnp.bfloat16),
        compiler_params=pltpu.CompilerParams(vmem_limit_bytes=48 << 20),
    )(*parts, cut(early[None], -1), cut(late[None], -1), cut(keep, 0.0)[:, None, :])


def edge_rows(value, axis, width, order=None):
    count, length = lax.axis_size(axis), value.shape[0] if order is None else value.shape[2]
    dim = 0 if order is None else 2
    up = [(i, (i + 1) % count) for i in range(count - 1)]
    down = [(j, i) for i, j in up]
    last = lax.slice_in_dim(value, length - width, length, axis=dim)
    leading = lax.slice_in_dim(value, 0, width, axis=dim)
    if order is not None:
        last, leading = jnp.transpose(last, order), jnp.transpose(leading, order)
    return lax.ppermute(last, axis, up), lax.ppermute(leading, axis, down)


def looks_kernel(pairs, planes_ref, top_ref, bottom_ref, band_ref, out_ref, box_ref):
    batch, strip, columns = planes_ref.shape[1:]
    band = band_ref[...]
    halves = columns // LANES
    rim = top_ref.shape[1]
    edges = []
    for c in range(2):
        along = jnp.dot(
            planes_ref[c].reshape(batch * strip, columns),
            band,
            preferred_element_type=jnp.float32,
        )
        for h in range(halves):
            box_ref[c, h] = along[:, h * LANES : (h + 1) * LANES]
        edges.append(
            [
                [jnp.dot(ref[c, i], band, preferred_element_type=jnp.float32) for i in range(rim)]
                for ref in (top_ref, bottom_ref)
            ]
        )
    spot = lax.broadcasted_iota(jnp.int32, (batch, LANES), 0) + pl.program_id(0) * batch
    valid = spot < pairs
    for h in range(halves):
        lanes = slice(h * LANES, (h + 1) * LANES)

        def row(c, r):
            if r < 0:
                return edges[c][0][r + rim][:, lanes]
            if r >= strip:
                return edges[c][1][r - strip][:, lanes]
            return box_ref[c, h, pl.ds(r, batch, stride=strip), :]

        lines = [[row(c, r) for r in range(-rim, -rim + 4)] for c in range(2)]
        for r in range(strip):
            boxed = []
            for c in range(2):
                lines[c].append(row(c, r + rim))
                a, b, d, e, f = lines[c]
                boxed.append((a + b) + (d + e) + f)
                lines[c].pop(0)
            power = boxed[0] * boxed[0] + boxed[1] * boxed[1]
            looks = boxed[1] * lax.rsqrt(jnp.maximum(power, 1.0))
            out_ref[r, :, lanes] = jnp.where(valid, looks, 0.0).astype(jnp.bfloat16)


def multilook(interferograms, top, bottom, width):
    pairs, strip, columns = interferograms.shape[1:]
    batch = width // (width // LANES + 2) if width % (width // LANES + 2) == 0 else LANES
    batch = batch if batch % 16 == 0 else LANES
    rim = top.shape[1]
    spots = np.arange(columns)
    band = (np.abs(spots[:, None] - spots[None, :]) <= 2).astype(ml_dtypes.bfloat16)
    edge = pl.BlockSpec((2, rim, batch, columns), lambda j: (0, 0, j, 0))
    return pl.pallas_call(
        functools.partial(looks_kernel, pairs),
        grid=(width // batch,),
        in_specs=[
            pl.BlockSpec((2, batch, strip, columns), lambda j: (0, j, 0, 0)),
            edge,
            edge,
            pl.BlockSpec((columns, columns), lambda j: (0, 0)),
        ],
        out_specs=pl.BlockSpec((strip, batch, columns), lambda j: (0, j, 0)),
        out_shape=jax.ShapeDtypeStruct((strip, width, columns), jnp.bfloat16),
        scratch_shapes=[
            pltpu.VMEM((2, columns // LANES, batch * strip, LANES), jnp.float32)
        ],
        compiler_params=pltpu.CompilerParams(vmem_limit_bytes=48 << 20),
    )(interferograms, top, bottom, jnp.asarray(band))


def series_kernel(half_ref, operator_ref, looks_ref, class_ref, out_ref):
    total = jnp.zeros((operator_ref.shape[1], looks_ref.shape[2]), jnp.float32)
    for q in range(operator_ref.shape[0]):
        solved = jnp.dot(operator_ref[q], looks_ref[0], preferred_element_type=jnp.float32)
        total = jnp.where(class_ref[0] == q, solved, total)
    out_ref[0] = total[: out_ref.shape[1]]


def invert(operators, looks, pattern_ids, half, rows):
    classes, dates, width = operators.shape
    columns = looks.shape[2]
    return pl.pallas_call(
        series_kernel,
        grid_spec=pltpu.PrefetchScalarGridSpec(
            num_scalar_prefetch=1,
            grid=(rows,),
            in_specs=[
                pl.BlockSpec((classes, dates, width), lambda r, h: (0, 0, 0)),
                pl.BlockSpec((1, width, columns), lambda r, h: (h[0] * rows + r, 0, 0)),
                pl.BlockSpec((1, 1, columns), lambda r, h: (h[0] * rows + r, 0, 0)),
            ],
            out_specs=pl.BlockSpec((1, DATES, columns), lambda r, h: (r, 0, 0)),
        ),
        out_shape=jax.ShapeDtypeStruct((rows, DATES, columns), jnp.float32),
        compiler_params=pltpu.CompilerParams(vmem_limit_bytes=48 << 20),
        cost_estimate=pl.CostEstimate(
            flops=2 * classes * dates * width * columns * rows,
            bytes_accessed=2 * rows * width * columns + 4 * rows * dates * columns,
            transcendentals=0,
        ),
    )(jnp.reshape(half, (1,)), operators, looks, pattern_ids[:, None, :])


def gauss_taps():
    spots = np.arange(-RADIUS, RADIUS + 1)
    raw = np.exp(-spots * spots / (2.0 * gauss_width * gauss_width))
    return raw / raw.sum()


def screen_kernel(taps, series_ref, before_ref, after_ref, high_ref, low_ref, out_ref):
    rows, tile, columns = series_ref.shape
    lines = [before_ref[i].astype(jnp.float32) for i in range(RADIUS)]
    lines += [series_ref[i] for i in range(rows)]
    lines += [after_ref[i].astype(jnp.float32) for i in range(RADIUS)]
    for r in range(rows):
        total = taps[RADIUS] * lines[r + RADIUS]
        for a in range(RADIUS):
            total += taps[a] * (lines[r + a] + lines[r + 2 * RADIUS - a])
        high = total.astype(jnp.bfloat16)
        low = (total - high.astype(jnp.float32)).astype(jnp.bfloat16)
        screen = jnp.dot(low, high_ref[...], preferred_element_type=jnp.float32)
        screen += jnp.dot(high, low_ref[...], preferred_element_type=jnp.float32)
        screen += jnp.dot(high, high_ref[...], preferred_element_type=jnp.float32)
        out_ref[r] = series_ref[r] - screen


def remove_screen(series, before, after):
    rows, dates, columns = series.shape
    taps = gauss_taps()
    spots = np.arange(columns)
    lag = spots[:, None] - spots[None, :]
    band = np.where(np.abs(lag) <= RADIUS, taps[np.clip(lag, -RADIUS, RADIUS) + RADIUS], 0.0)
    band = band.astype(np.float32)
    high = band.astype(ml_dtypes.bfloat16)
    low = (band - high.astype(np.float32)).astype(ml_dtypes.bfloat16)
    tile = 64
    piece = lambda count: pl.BlockSpec((count, tile, columns), lambda t: (0, t, 0))
    square = pl.BlockSpec((columns, columns), lambda t: (0, 0))
    return pl.pallas_call(
        functools.partial(screen_kernel, [float(x) for x in taps]),
        grid=(-(-dates // tile),),
        in_specs=[piece(rows), piece(RADIUS), piece(RADIUS), square, square],
        out_specs=piece(rows),
        out_shape=jax.ShapeDtypeStruct(series.shape, jnp.float32),
        compiler_params=pltpu.CompilerParams(vmem_limit_bytes=48 << 20),
    )(series, before, after, jnp.asarray(high), jnp.asarray(low))


def body(interferograms, pair_dates, mask_table, gap_dates, pattern_ids):
    pairs, strip = interferograms.shape[1:3]
    shares = lax.axis_size("pairs")
    place = lax.axis_index("pairs")
    my_rows = strip // shares
    width = round_up(pairs, LANES)
    top, bottom = edge_rows(interferograms, "rows", 2, (0, 2, 1, 3))
    operators = build_operators(pair_dates, mask_table, gap_dates, (place, shares), width)
    looks = multilook(interferograms, top, bottom, width)
    series = None
    for turn in range(shares - 1, -1, -1):
        half = (place + turn) % shares
        part = invert(operators, looks, pattern_ids, half, my_rows)
        if turn:
            part = lax.ppermute(part, "pairs", [(i, (i + turn) % shares) for i in range(shares)])
        series = part if series is None else series + part
    before, after = edge_rows_bf16(series)
    return remove_screen(series, before, after)


def edge_rows_bf16(series):
    return edge_rows(series.astype(jnp.bfloat16), ("rows", "pairs"), RADIUS)


def solution(mesh):
    placed = (
        P(None, "pairs", ("blocks", "rows"), None),
        P(),
        P(),
        P(),
        P(("blocks", "rows"), None),
    )
    return jax.shard_map(
        body,
        mesh=mesh,
        in_specs=placed,
        out_specs=P(("blocks", "rows", "pairs"), None, None),
        check_vma=False,
    )
```

```python
import functools

import jax
import ml_dtypes
import numpy as np
import jax.numpy as jnp
from jax import lax
from jax.experimental import pallas as pl
from jax.experimental.pallas import tpu as pltpu
from jax.sharding import PartitionSpec as P

DATES = 300
NPAT = 4
SPAN = 5
RADIUS = 6
LANES = 128
BLOCKS = DATES // SPAN
BLOCKS_PAD = 64
DATES_PAD = 304
LEVELS = 6
RIM = 32
SUB = 8
WIDE = 384


damping = 0.5
corr_length = 10.0
gauss_width = 2.0


def round_up(value, unit):
    return -(-value // unit) * unit


def block_matmul(left, right, transposed=False):
    size = len(left)
    out = []
    for a in range(size):
        row = []
        for b in range(size):
            total = None
            for m in range(size):
                term = left[a][m] * (right[b][m] if transposed else right[m][b])
                total = term if total is None else total + term
            row.append(total)
        out.append(row)
    return out


def block_inverse(matrix):
    size = len(matrix)
    work = [list(row) for row in matrix]
    for k in range(size):
        pivot = 1.0 / work[k][k]
        work[k] = [pivot if j == k else work[k][j] * pivot for j in range(size)]
        for i in range(size):
            if i != k:
                factor = work[i][k]
                work[i] = [
                    -factor * pivot if j == k else work[i][j] - factor * work[k][j]
                    for j in range(size)
                ]
    return work


def moved(blocks, shift):
    return [[pltpu.roll(item, shift % LANES, 1) for item in row] for row in blocks]


def nearest_weights(gap_ref, near_ref):
    gaps = gap_ref[...]
    shape = near_ref.shape[1:]
    dates = lax.broadcasted_iota(jnp.int32, shape, 1)
    gapped = jnp.zeros(shape, jnp.float32)
    for g in range(gaps.shape[1]):
        gapped = jnp.where(gaps[:, g : g + 1] == dates, 1.0, gapped)
    seen = (gapped < 0.5) & (dates < DATES)
    day = dates.astype(jnp.float32)
    left = jnp.where(seen, day, -1.0)
    right = jnp.where(seen, day, float(DATES))
    step = 1
    while step <= gaps.shape[1]:
        left = jnp.maximum(left, jnp.where(dates >= step, pltpu.roll(left, step, 1), -1.0))
        right = jnp.minimum(
            right,
            jnp.where(
                dates < shape[1] - step, pltpu.roll(right, shape[1] - step, 1), float(DATES)
            ),
        )
        step *= 2
    ahead = (right - day) / corr_length
    behind = (day - left) / corr_length
    sinh = lambda x: 0.5 * (jnp.exp(x) - jnp.exp(-x))
    whole = sinh(jnp.maximum(ahead + behind, 1.0 / corr_length))
    no_left = left < 0.0
    no_right = right >= float(DATES)
    from_left = jnp.where(no_right, jnp.exp(-behind), sinh(ahead) / whole)
    from_right = jnp.where(no_left, jnp.exp(-ahead), sinh(behind) / whole)
    near_ref[0] = left
    near_ref[1] = right
    near_ref[2] = jnp.where((gapped > 0.5) & ~no_left, from_left, 0.0)
    near_ref[3] = jnp.where((gapped > 0.5) & ~no_right, from_right, 0.0)


def reduction_kernel(keep_ref, early_ref, late_ref, gap_ref, coef_ref, near_ref):
    nearest_weights(gap_ref, near_ref)
    early = early_ref[...]
    span = late_ref[...] - early
    keep = keep_ref[...]
    classes = keep.shape[0]
    picked = jnp.concatenate(
        [jnp.where(span == d, keep, 0.0) for d in range(1, SPAN + 1)], axis=0
    ).astype(jnp.bfloat16)
    count = {}
    for a in range(SPAN):
        date = SPAN * lax.broadcasted_iota(jnp.int32, (LANES, early.shape[1]), 0) + a
        hot = jnp.where(date == early, 1.0, 0.0).astype(jnp.bfloat16)
        counts = lax.dot_general(
            picked, hot, (((1,), (1,)), ((), ())), preferred_element_type=jnp.float32
        )
        for d in range(1, SPAN + 1):
            count[d, a] = counts[(d - 1) * classes : d * classes]
    diagonal, upper = [], []
    for a in range(SPAN):
        total = damping
        for d in range(1, SPAN + 1):
            total = total + count[d, a]
            if a >= d:
                total = total + count[d, a - d]
            else:
                total = total + pltpu.roll(count[d, a - d + SPAN], 1, 1)
        diagonal.append(
            [total if b == a else -count[abs(b - a), min(a, b)] for b in range(SPAN)]
        )
        zero = jnp.zeros_like(total)
        upper.append([-count[SPAN + b - a, a] if b <= a else zero for b in range(SPAN)])
    slot = 0
    step = 1
    while step < BLOCKS:
        inverse = block_inverse(diagonal)
        flipped = [list(row) for row in zip(*upper)]
        below = block_matmul(flipped, inverse)
        gamma = [[-x for x in row] for row in block_matmul(upper, moved(inverse, -step))]
        alpha = [[-x for x in row] for row in moved(below, step)]
        first = moved(block_matmul(below, upper), step)
        second = block_matmul(gamma, upper, transposed=True)
        diagonal = [
            [diagonal[a][b] - first[a][b] + second[a][b] for b in range(SPAN)]
            for a in range(SPAN)
        ]
        upper = block_matmul(gamma, moved(upper, -step))
        for part in (alpha, gamma):
            for row in part:
                for item in row:
                    coef_ref[slot] = item
                    slot += 1
        step *= 2
    for row in block_inverse(diagonal):
        for item in row:
            coef_ref[slot] = item
            slot += 1


def reaching(step, first):
    low = SPAN * (first - (step - 1))
    high = SPAN * (first + SUB + step - 1)
    return [t for t in range(WIDE // LANES) if high > t * LANES and low < (t + 1) * LANES]


def inverse_kernel(coef_ref, mix_ref, early_ref, late_ref, keep_ref, out_ref, state_ref, flat_ref):
    state_ref[...] = jnp.zeros_like(state_ref)
    column = lax.broadcasted_iota(jnp.int32, (BLOCKS_PAD, WIDE), 1)
    date = SPAN * lax.broadcasted_iota(jnp.int32, (BLOCKS_PAD, WIDE), 0)
    for a in range(SPAN):
        state_ref[0, a, RIM : RIM + BLOCKS_PAD] = jnp.where(date + a == column, 1.0, 0.0)
    slot = 0
    step = 1
    turn = 0
    square = SPAN * SPAN
    while step < BLOCKS:
        for first in range(0, BLOCKS_PAD, SUB):
            rows = slice(RIM + first, RIM + first + SUB)
            coef = coef_ref[0, first : first + SUB]
            sides = []
            if first + SUB > step:
                sides.append((slot, -step))
            if first + step < BLOCKS:
                sides.append((slot + square, step))
            tiles = [slice(t * LANES, (t + 1) * LANES) for t in reaching(2 * step, first)]
            fresh = [[state_ref[turn, a, rows, lanes] for lanes in tiles] for a in range(SPAN)]
            for base, shift in sides:
                near = slice(RIM + first + shift, RIM + first + shift + SUB)
                for b in range(SPAN):
                    other = [state_ref[turn, b, near, lanes] for lanes in tiles]
                    for a in range(SPAN):
                        at = base + a * SPAN + b
                        factor = jnp.broadcast_to(coef[:, at : at + 1], (SUB, LANES))
                        fresh[a] = [x + factor * y for x, y in zip(fresh[a], other)]
            for a in range(SPAN):
                for lanes, value in zip(tiles, fresh[a]):
                    state_ref[1 - turn, a, rows, lanes] = value
        slot += 2 * square
        step *= 2
        turn = 1 - turn
    for first in range(0, BLOCKS_PAD, SUB):
        coef = coef_ref[0, first : first + SUB]
        rows = slice(RIM + first, RIM + first + SUB)
        last = [state_ref[turn, b, rows] for b in range(SPAN)]
        for a in range(SPAN):
            total = None
            for b in range(SPAN):
                at = slot + a * SPAN + b
                term = coef[:, at : at + 1] * last[b]
                total = term if total is None else total + term
            flat_ref[a * BLOCKS_PAD + first : a * BLOCKS_PAD + first + SUB] = total
    mixed = jnp.dot(
        mix_ref[0],
        flat_ref[...],
        precision=lax.Precision.HIGHEST,
        preferred_element_type=jnp.float32,
    )
    high = mixed.astype(jnp.bfloat16)
    rest = mixed - high.astype(jnp.float32)
    mid = rest.astype(jnp.bfloat16)
    low = (rest - mid.astype(jnp.float32)).astype(jnp.bfloat16)
    date = lax.broadcasted_iota(jnp.int32, (WIDE, early_ref.shape[1]), 0)
    plus = jnp.where(date == late_ref[...], 1.0, 0.0)
    minus = jnp.where(date == early_ref[...], 1.0, 0.0)
    incidence = (plus - minus).astype(jnp.bfloat16)
    total = jnp.dot(low, incidence, preferred_element_type=jnp.float32)
    total += jnp.dot(mid, incidence, preferred_element_type=jnp.float32)
    total += jnp.dot(high, incidence, preferred_element_type=jnp.float32)
    out_ref[0] = (total * keep_ref[0]).astype(jnp.bfloat16)


def mixing_matrix(near):
    left, right, from_left, from_right = (near[i, :, :, None] for i in range(4))
    place = jnp.arange(SPAN * BLOCKS_PAD, dtype=jnp.int32)
    source = SPAN * (place % BLOCKS_PAD) + place // BLOCKS_PAD
    source = jnp.where((source < DATES) & (place % BLOCKS_PAD < BLOCKS), source, -2)
    source = source.astype(jnp.float32)
    dates = jnp.arange(near.shape[2], dtype=jnp.int32).astype(jnp.float32)
    mix = jnp.where(source == dates[:, None], 1.0, 0.0)[None]
    mix = mix + jnp.where(source == left, from_left, 0.0)
    return mix + jnp.where(source == right, from_right, 0.0)


def build_operators(pair_dates, mask_table, gap_dates, own, width):
    classes, pairs = mask_table.shape
    early, late = pair_dates[:, 0], pair_dates[:, 1]
    lost = jnp.any(
        (gap_dates[:, :, None] == early) | (gap_dates[:, :, None] == late), axis=1
    )
    keep = jnp.where(lost, 0.0, mask_table.astype(jnp.float32))
    padded = round_up(pairs, LANES)
    keep_all = jnp.pad(keep, ((0, round_up(classes, 8) - classes), (0, padded - pairs)))
    early_all = jnp.pad(early[None], ((0, 0), (0, padded - pairs)), constant_values=-1)
    late_all = jnp.pad(late[None], ((0, 0), (0, padded - pairs)), constant_values=-1)
    slots = (2 * LEVELS + 1) * SPAN * SPAN
    extra = keep_all.shape[0] - classes
    gap_all = jnp.pad(gap_dates, ((0, extra), (0, 0)), constant_values=-1)
    coef, near = pl.pallas_call(
        reduction_kernel,
        out_shape=[
            jax.ShapeDtypeStruct((slots, keep_all.shape[0], LANES), jnp.float32),
            jax.ShapeDtypeStruct((4, keep_all.shape[0], WIDE), jnp.float32),
        ],
        compiler_params=pltpu.CompilerParams(vmem_limit_bytes=48 << 20),
        cost_estimate=pl.CostEstimate(flops=1 << 32, bytes_accessed=1 << 20, transcendentals=0),
    )(keep_all, early_all, late_all, gap_all)
    coef = jnp.transpose(coef[:, :classes, :BLOCKS_PAD], (1, 2, 0))
    mix = mixing_matrix(near[:, :classes, :DATES_PAD])
    count = pairs // own[1]
    begin = own[0] * count
    cut = lambda value, fill: jnp.pad(
        lax.dynamic_slice_in_dim(value, begin, count, 1),
        ((0, 0), (0, width - count)),
        constant_values=fill,
    )
    line = pl.BlockSpec((1, width), lambda q: (0, 0))
    return pl.pallas_call(
        inverse_kernel,
        grid=(classes,),
        in_specs=[
            pl.BlockSpec((1, BLOCKS_PAD, slots), lambda q: (q, 0, 0)),
            pl.BlockSpec((1, DATES_PAD, SPAN * BLOCKS_PAD), lambda q: (q, 0, 0)),
            line,
            line,
            pl.BlockSpec((1, 1, width), lambda q: (q, 0, 0)),
        ],
        out_specs=pl.BlockSpec((1, DATES_PAD, width), lambda q: (q, 0, 0)),
        out_shape=jax.ShapeDtypeStruct((classes, DATES_PAD, width), jnp.bfloat16),
        scratch_shapes=[
            pltpu.VMEM((2, SPAN, BLOCKS_PAD + 2 * RIM, WIDE), jnp.float32),
            pltpu.VMEM((SPAN * BLOCKS_PAD, WIDE), jnp.float32),
        ],
        compiler_params=pltpu.CompilerParams(vmem_limit_bytes=48 << 20),
        cost_estimate=pl.CostEstimate(flops=3 << 33, bytes_accessed=4 << 20, transcendentals=0),
    )(coef, mix, cut(early[None], -1), cut(late[None], -1), cut(keep, 0.0)[:, None, :])


def edge_rows(value, axis, width, order=None):
    count, length = lax.axis_size(axis), value.shape[0] if order is None else value.shape[2]
    dim = 0 if order is None else 2
    up = [(i, (i + 1) % count) for i in range(count - 1)]
    down = [(j, i) for i, j in up]
    last = lax.slice_in_dim(value, length - width, length, axis=dim)
    leading = lax.slice_in_dim(value, 0, width, axis=dim)
    if order is not None:
        last, leading = jnp.transpose(last, order), jnp.transpose(leading, order)
    return lax.ppermute(last, axis, up), lax.ppermute(leading, axis, down)


def from_box(boxed, valid):
    power = boxed[0] * boxed[0] + boxed[1] * boxed[1]
    looks = boxed[1] * lax.rsqrt(jnp.maximum(power, 1.0))
    return jnp.where(valid, looks, 0.0).astype(jnp.bfloat16)


def within(pairs, batch, lanes):
    spot = lax.broadcasted_iota(jnp.int32, (batch, lanes), 0) + pl.program_id(0) * batch
    return spot < pairs


def inner_kernel(pairs, planes_ref, band_ref, out_ref, rim_ref, box_ref):
    batch, strip, columns = planes_ref.shape[1:]
    halves = columns // LANES
    for c in range(2):
        along = jnp.dot(
            planes_ref[c].reshape(batch * strip, columns),
            band_ref[...],
            preferred_element_type=jnp.float32,
        )
        for h in range(halves):
            box_ref[c, h] = along[:, h * LANES : (h + 1) * LANES]
    valid = within(pairs, batch, LANES)
    for h in range(halves):
        lanes = slice(h * LANES, (h + 1) * LANES)
        lines = [
            [box_ref[c, h, pl.ds(r, batch, stride=strip), :] for r in range(4)] for c in range(2)
        ]
        for c in range(2):
            near = (lines[c][0] + lines[c][1]) + lines[c][2]
            rim_ref[c, 0, :, lanes] = near
            rim_ref[c, 1, :, lanes] = near + lines[c][3]
        for r in range(2, strip - 2):
            boxed = []
            for c in range(2):
                lines[c].append(box_ref[c, h, pl.ds(r + 2, batch, stride=strip), :])
                a, b, d, e, f = lines[c]
                boxed.append((a + b) + (d + e) + f)
                lines[c].pop(0)
            out_ref[r - 2, :, lanes] = from_box(boxed, valid)
        for c in range(2):
            near = (lines[c][1] + lines[c][2]) + lines[c][3]
            rim_ref[c, 2, :, lanes] = near + lines[c][0]
            rim_ref[c, 3, :, lanes] = near


def outer_kernel(pairs, rim_ref, top_ref, bottom_ref, band_ref, out_ref):
    batch, columns = rim_ref.shape[2:]
    band = band_ref[...]
    valid = within(pairs, batch, columns)
    sums = []
    for c in range(2):
        above = [
            jnp.dot(top_ref[c, i], band, preferred_element_type=jnp.float32) for i in range(2)
        ]
        below = [
            jnp.dot(bottom_ref[c, i], band, preferred_element_type=jnp.float32) for i in range(2)
        ]
        sums.append(
            [
                rim_ref[c, 0] + (above[0] + above[1]),
                rim_ref[c, 1] + above[1],
                rim_ref[c, 2] + below[0],
                rim_ref[c, 3] + (below[0] + below[1]),
            ]
        )
    for r in range(4):
        out_ref[r] = from_box([sums[0][r], sums[1][r]], valid)


def pick_batch(width):
    return 96 if width % 96 == 0 else LANES


def column_band(columns):
    spots = np.arange(columns)
    return jnp.asarray(
        (np.abs(spots[:, None] - spots[None, :]) <= 2).astype(ml_dtypes.bfloat16)
    )


def multilook_inner(interferograms, width):
    pairs, strip, columns = interferograms.shape[1:]
    batch = pick_batch(width)
    return pl.pallas_call(
        functools.partial(inner_kernel, pairs),
        grid=(width // batch,),
        in_specs=[
            pl.BlockSpec((2, batch, strip, columns), lambda j: (0, j, 0, 0)),
            pl.BlockSpec((columns, columns), lambda j: (0, 0)),
        ],
        out_specs=[
            pl.BlockSpec((strip - 4, batch, columns), lambda j: (0, j, 0)),
            pl.BlockSpec((2, 4, batch, columns), lambda j: (0, 0, j, 0)),
        ],
        out_shape=[
            jax.ShapeDtypeStruct((strip - 4, width, columns), jnp.bfloat16),
            jax.ShapeDtypeStruct((2, 4, width, columns), jnp.float32),
        ],
        scratch_shapes=[
            pltpu.VMEM((2, columns // LANES, batch * strip, LANES), jnp.float32)
        ],
        compiler_params=pltpu.CompilerParams(vmem_limit_bytes=40 << 20),
        cost_estimate=pl.CostEstimate(flops=3 << 33, bytes_accessed=24 << 20, transcendentals=0),
    )(interferograms, column_band(columns))


def multilook_outer(rims, top, bottom, pairs):
    width, columns = rims.shape[2:]
    batch = pick_batch(width)
    edge = pl.BlockSpec((2, 2, batch, columns), lambda j: (0, 0, j, 0))
    return pl.pallas_call(
        functools.partial(outer_kernel, pairs),
        grid=(width // batch,),
        in_specs=[
            pl.BlockSpec((2, 4, batch, columns), lambda j: (0, 0, j, 0)),
            edge,
            edge,
            pl.BlockSpec((columns, columns), lambda j: (0, 0)),
        ],
        out_specs=pl.BlockSpec((4, batch, columns), lambda j: (0, j, 0)),
        out_shape=jax.ShapeDtypeStruct((4, width, columns), jnp.bfloat16),
        compiler_params=pltpu.CompilerParams(vmem_limit_bytes=40 << 20),
    )(rims, top, bottom, column_band(columns))


def series_kernel(half_ref, operator_ref, looks_ref, class_ref, out_ref):
    total = jnp.zeros((operator_ref.shape[1], looks_ref.shape[2]), jnp.float32)
    for q in range(operator_ref.shape[0]):
        solved = jnp.dot(operator_ref[q], looks_ref[0], preferred_element_type=jnp.float32)
        total = jnp.where(class_ref[0] == q, solved, total)
    out_ref[0] = total


def invert(operators, looks, pattern_ids, half, rows):
    classes, dates, width = operators.shape
    columns = looks.shape[2]
    return pl.pallas_call(
        series_kernel,
        grid_spec=pltpu.PrefetchScalarGridSpec(
            num_scalar_prefetch=1,
            grid=(rows,),
            in_specs=[
                pl.BlockSpec((classes, dates, width), lambda r, h: (0, 0, 0)),
                pl.BlockSpec((1, width, columns), lambda r, h: (h[0] * rows + r, 0, 0)),
                pl.BlockSpec((1, 1, columns), lambda r, h: (h[0] * rows + r, 0, 0)),
            ],
            out_specs=pl.BlockSpec((1, dates, columns), lambda r, h: (r, 0, 0)),
        ),
        out_shape=jax.ShapeDtypeStruct((rows, dates, columns), jnp.float32),
        compiler_params=pltpu.CompilerParams(vmem_limit_bytes=48 << 20),
        cost_estimate=pl.CostEstimate(
            flops=2 * classes * dates * width * columns * rows,
            bytes_accessed=2 * rows * width * columns + 4 * rows * dates * columns,
            transcendentals=0,
        ),
    )(jnp.reshape(half, (1,)), operators, looks, pattern_ids[:, None, :])


def gauss_taps():
    spots = np.arange(-RADIUS, RADIUS + 1)
    raw = np.exp(-spots * spots / (2.0 * gauss_width * gauss_width))
    return raw / raw.sum()


def screen_kernel(taps, series_ref, before_ref, after_ref, high_ref, low_ref, out_ref):
    rows, tile, columns = series_ref.shape
    lines = [before_ref[i].astype(jnp.float32) for i in range(RADIUS)]
    lines += [series_ref[i] for i in range(rows)]
    lines += [after_ref[i].astype(jnp.float32) for i in range(RADIUS)]
    for r in range(rows):
        total = taps[RADIUS] * lines[r + RADIUS]
        for a in range(RADIUS):
            total += taps[a] * (lines[r + a] + lines[r + 2 * RADIUS - a])
        high = total.astype(jnp.bfloat16)
        low = (total - high.astype(jnp.float32)).astype(jnp.bfloat16)
        screen = jnp.dot(low, high_ref[...], preferred_element_type=jnp.float32)
        screen += jnp.dot(high, low_ref[...], preferred_element_type=jnp.float32)
        screen += jnp.dot(high, high_ref[...], preferred_element_type=jnp.float32)
        out_ref[r] = series_ref[r] - screen


def remove_screen(series, before, after):
    rows, dates, columns = series.shape
    taps = gauss_taps()
    spots = np.arange(columns)
    lag = spots[:, None] - spots[None, :]
    band = np.where(np.abs(lag) <= RADIUS, taps[np.clip(lag, -RADIUS, RADIUS) + RADIUS], 0.0)
    band = band.astype(np.float32)
    high = band.astype(ml_dtypes.bfloat16)
    low = (band - high.astype(np.float32)).astype(ml_dtypes.bfloat16)
    tile = 64
    piece = lambda count: pl.BlockSpec((count, tile, columns), lambda t: (0, t, 0))
    square = pl.BlockSpec((columns, columns), lambda t: (0, 0))
    return pl.pallas_call(
        functools.partial(screen_kernel, [float(x) for x in taps]),
        grid=(-(-dates // tile),),
        in_specs=[piece(rows), piece(RADIUS), piece(RADIUS), square, square],
        out_specs=piece(rows),
        out_shape=jax.ShapeDtypeStruct((rows, DATES, columns), jnp.float32),
        compiler_params=pltpu.CompilerParams(vmem_limit_bytes=48 << 20),
    )(series, before, after, jnp.asarray(high), jnp.asarray(low))


def body(interferograms, pair_dates, mask_table, gap_dates, pattern_ids):
    pairs, strip = interferograms.shape[1:3]
    shares = lax.axis_size("pairs")
    place = lax.axis_index("pairs")
    width = round_up(pairs, LANES)
    top, bottom = edge_rows(interferograms, "rows", 2, (0, 2, 1, 3))
    operators = build_operators(pair_dates, mask_table, gap_dates, (place, shares), width)
    inner_looks, rims = multilook_inner(interferograms, width)
    inner_ids = pattern_ids[2 : strip - 2]
    outer_ids = jnp.concatenate([pattern_ids[:2], pattern_ids[strip - 2 :]])
    across = [(i, 1 - i) for i in range(shares)]
    inner_away = invert(operators, inner_looks, inner_ids, 1 - place, strip // 2 - 2)
    inner_got = lax.ppermute(inner_away, "pairs", across)
    inner_own = invert(operators, inner_looks, inner_ids, place, strip // 2 - 2)
    outer_looks = multilook_outer(rims, top, bottom, pairs)
    outer_away = invert(operators, outer_looks, outer_ids, 1 - place, 2)
    outer_got = lax.ppermute(outer_away, "pairs", across)
    outer_own = invert(operators, outer_looks, outer_ids, place, 2)
    inner = inner_own + inner_got
    outer = outer_own + outer_got
    series = jnp.where(
        place == 0,
        jnp.concatenate([outer, inner]),
        jnp.concatenate([inner, outer]),
    )
    before, after = edge_rows_bf16(series)
    return remove_screen(series, before, after)


def edge_rows_bf16(series):
    return edge_rows(series.astype(jnp.bfloat16), ("rows", "pairs"), RADIUS)


def solution(mesh):
    placed = (
        P(None, "pairs", ("blocks", "rows"), None),
        P(),
        P(),
        P(),
        P(("blocks", "rows"), None),
    )
    return jax.shard_map(
        body,
        mesh=mesh,
        in_specs=placed,
        out_specs=P(("blocks", "rows", "pairs"), None, None),
        check_vma=False,
    )
```

```python
import functools

import jax
import ml_dtypes
import numpy as np
import jax.numpy as jnp
from jax import lax
from jax.experimental import pallas as pl
from jax.experimental.pallas import tpu as pltpu
from jax.sharding import PartitionSpec as P

DATES = 300
NPAT = 4
SPAN = 5
RADIUS = 6
LANES = 128
BLOCKS = DATES // SPAN
BLOCKS_PAD = 64
DATES_PAD = 304
LEVELS = 6
RIM = 32
SUB = 8
WIDE = 384


damping = 0.5
corr_length = 10.0
gauss_width = 2.0


def round_up(value, unit):
    return -(-value // unit) * unit


def block_matmul(left, right, transposed=False):
    size = len(left)
    out = []
    for a in range(size):
        row = []
        for b in range(size):
            total = None
            for m in range(size):
                term = left[a][m] * (right[b][m] if transposed else right[m][b])
                total = term if total is None else total + term
            row.append(total)
        out.append(row)
    return out


def block_inverse(matrix):
    size = len(matrix)
    work = [list(row) for row in matrix]
    for k in range(size):
        pivot = 1.0 / work[k][k]
        work[k] = [pivot if j == k else work[k][j] * pivot for j in range(size)]
        for i in range(size):
            if i != k:
                factor = work[i][k]
                work[i] = [
                    -factor * pivot if j == k else work[i][j] - factor * work[k][j]
                    for j in range(size)
                ]
    return work


def moved(blocks, shift):
    return [[pltpu.roll(item, shift % LANES, 1) for item in row] for row in blocks]


def nearest_weights(gap_ref, near_ref):
    gaps = gap_ref[...]
    shape = near_ref.shape[1:]
    dates = lax.broadcasted_iota(jnp.int32, shape, 1)
    gapped = jnp.zeros(shape, jnp.float32)
    for g in range(gaps.shape[1]):
        gapped = jnp.where(gaps[:, g : g + 1] == dates, 1.0, gapped)
    seen = (gapped < 0.5) & (dates < DATES)
    day = dates.astype(jnp.float32)
    left = jnp.where(seen, day, -1.0)
    right = jnp.where(seen, day, float(DATES))
    step = 1
    while step <= gaps.shape[1]:
        left = jnp.maximum(left, jnp.where(dates >= step, pltpu.roll(left, step, 1), -1.0))
        right = jnp.minimum(
            right,
            jnp.where(
                dates < shape[1] - step, pltpu.roll(right, shape[1] - step, 1), float(DATES)
            ),
        )
        step *= 2
    ahead = (right - day) / corr_length
    behind = (day - left) / corr_length
    sinh = lambda x: 0.5 * (jnp.exp(x) - jnp.exp(-x))
    whole = sinh(jnp.maximum(ahead + behind, 1.0 / corr_length))
    no_left = left < 0.0
    no_right = right >= float(DATES)
    from_left = jnp.where(no_right, jnp.exp(-behind), sinh(ahead) / whole)
    from_right = jnp.where(no_left, jnp.exp(-ahead), sinh(behind) / whole)
    near_ref[0] = left
    near_ref[1] = right
    near_ref[2] = jnp.where((gapped > 0.5) & ~no_left, from_left, 0.0)
    near_ref[3] = jnp.where((gapped > 0.5) & ~no_right, from_right, 0.0)


def reduction_kernel(keep_ref, early_ref, late_ref, gap_ref, coef_ref, near_ref):
    nearest_weights(gap_ref, near_ref)
    early = early_ref[...]
    span = late_ref[...] - early
    keep = keep_ref[...]
    classes = keep.shape[0]
    picked = jnp.concatenate(
        [jnp.where(span == d, keep, 0.0) for d in range(1, SPAN + 1)], axis=0
    ).astype(jnp.bfloat16)
    count = {}
    for a in range(SPAN):
        date = SPAN * lax.broadcasted_iota(jnp.int32, (LANES, early.shape[1]), 0) + a
        hot = jnp.where(date == early, 1.0, 0.0).astype(jnp.bfloat16)
        counts = lax.dot_general(
            picked, hot, (((1,), (1,)), ((), ())), preferred_element_type=jnp.float32
        )
        for d in range(1, SPAN + 1):
            count[d, a] = counts[(d - 1) * classes : d * classes]
    diagonal, upper = [], []
    for a in range(SPAN):
        total = damping
        for d in range(1, SPAN + 1):
            total = total + count[d, a]
            if a >= d:
                total = total + count[d, a - d]
            else:
                total = total + pltpu.roll(count[d, a - d + SPAN], 1, 1)
        diagonal.append(
            [total if b == a else -count[abs(b - a), min(a, b)] for b in range(SPAN)]
        )
        zero = jnp.zeros_like(total)
        upper.append([-count[SPAN + b - a, a] if b <= a else zero for b in range(SPAN)])
    slot = 0
    step = 1
    while step < BLOCKS:
        inverse = block_inverse(diagonal)
        flipped = [list(row) for row in zip(*upper)]
        below = block_matmul(flipped, inverse)
        gamma = [[-x for x in row] for row in block_matmul(upper, moved(inverse, -step))]
        alpha = [[-x for x in row] for row in moved(below, step)]
        first = moved(block_matmul(below, upper), step)
        second = block_matmul(gamma, upper, transposed=True)
        diagonal = [
            [diagonal[a][b] - first[a][b] + second[a][b] for b in range(SPAN)]
            for a in range(SPAN)
        ]
        upper = block_matmul(gamma, moved(upper, -step))
        for part in (alpha, gamma):
            for row in part:
                for item in row:
                    coef_ref[slot] = item
                    slot += 1
        step *= 2
    for row in block_inverse(diagonal):
        for item in row:
            coef_ref[slot] = item
            slot += 1


def reaching(step, first):
    low = SPAN * (first - (step - 1))
    high = SPAN * (first + SUB + step - 1)
    return [t for t in range(WIDE // LANES) if high > t * LANES and low < (t + 1) * LANES]


def inverse_kernel(coef_ref, mix_ref, early_ref, late_ref, keep_ref, out_ref, state_ref, flat_ref):
    state_ref[...] = jnp.zeros_like(state_ref)
    column = lax.broadcasted_iota(jnp.int32, (BLOCKS_PAD, WIDE), 1)
    date = SPAN * lax.broadcasted_iota(jnp.int32, (BLOCKS_PAD, WIDE), 0)
    for a in range(SPAN):
        state_ref[0, a, RIM : RIM + BLOCKS_PAD] = jnp.where(date + a == column, 1.0, 0.0)
    slot = 0
    step = 1
    turn = 0
    square = SPAN * SPAN
    while step < BLOCKS:
        for first in range(0, BLOCKS_PAD, SUB):
            rows = slice(RIM + first, RIM + first + SUB)
            coef = coef_ref[0, first : first + SUB]
            sides = []
            if first + SUB > step:
                sides.append((slot, -step))
            if first + step < BLOCKS:
                sides.append((slot + square, step))
            tiles = [slice(t * LANES, (t + 1) * LANES) for t in reaching(2 * step, first)]
            fresh = [[state_ref[turn, a, rows, lanes] for lanes in tiles] for a in range(SPAN)]
            for base, shift in sides:
                near = slice(RIM + first + shift, RIM + first + shift + SUB)
                for b in range(SPAN):
                    other = [state_ref[turn, b, near, lanes] for lanes in tiles]
                    for a in range(SPAN):
                        at = base + a * SPAN + b
                        factor = jnp.broadcast_to(coef[:, at : at + 1], (SUB, LANES))
                        fresh[a] = [x + factor * y for x, y in zip(fresh[a], other)]
            for a in range(SPAN):
                for lanes, value in zip(tiles, fresh[a]):
                    state_ref[1 - turn, a, rows, lanes] = value
        slot += 2 * square
        step *= 2
        turn = 1 - turn
    for first in range(0, BLOCKS_PAD, SUB):
        coef = coef_ref[0, first : first + SUB]
        rows = slice(RIM + first, RIM + first + SUB)
        last = [state_ref[turn, b, rows] for b in range(SPAN)]
        for a in range(SPAN):
            total = None
            for b in range(SPAN):
                at = slot + a * SPAN + b
                term = coef[:, at : at + 1] * last[b]
                total = term if total is None else total + term
            flat_ref[a * BLOCKS_PAD + first : a * BLOCKS_PAD + first + SUB] = total
    mixed = jnp.dot(
        mix_ref[0],
        flat_ref[...],
        precision=lax.Precision.HIGHEST,
        preferred_element_type=jnp.float32,
    )
    high = mixed.astype(jnp.bfloat16)
    rest = mixed - high.astype(jnp.float32)
    mid = rest.astype(jnp.bfloat16)
    low = (rest - mid.astype(jnp.float32)).astype(jnp.bfloat16)
    date = lax.broadcasted_iota(jnp.int32, (WIDE, early_ref.shape[1]), 0)
    plus = jnp.where(date == late_ref[...], 1.0, 0.0)
    minus = jnp.where(date == early_ref[...], 1.0, 0.0)
    incidence = (plus - minus).astype(jnp.bfloat16)
    total = jnp.dot(low, incidence, preferred_element_type=jnp.float32)
    total += jnp.dot(mid, incidence, preferred_element_type=jnp.float32)
    total += jnp.dot(high, incidence, preferred_element_type=jnp.float32)
    out_ref[0] = (total * keep_ref[0]).astype(jnp.bfloat16)


def mixing_matrix(near):
    left, right, from_left, from_right = (near[i, :, :, None] for i in range(4))
    place = jnp.arange(SPAN * BLOCKS_PAD, dtype=jnp.int32)
    source = SPAN * (place % BLOCKS_PAD) + place // BLOCKS_PAD
    source = jnp.where((source < DATES) & (place % BLOCKS_PAD < BLOCKS), source, -2)
    source = source.astype(jnp.float32)
    dates = jnp.arange(near.shape[2], dtype=jnp.int32).astype(jnp.float32)
    mix = jnp.where(source == dates[:, None], 1.0, 0.0)[None]
    mix = mix + jnp.where(source == left, from_left, 0.0)
    return mix + jnp.where(source == right, from_right, 0.0)


def build_operators(pair_dates, mask_table, gap_dates, own, width):
    classes, pairs = mask_table.shape
    early, late = pair_dates[:, 0], pair_dates[:, 1]
    lost = jnp.any(
        (gap_dates[:, :, None] == early) | (gap_dates[:, :, None] == late), axis=1
    )
    keep = jnp.where(lost, 0.0, mask_table.astype(jnp.float32))
    padded = round_up(pairs, LANES)
    keep_all = jnp.pad(keep, ((0, round_up(classes, 8) - classes), (0, padded - pairs)))
    early_all = jnp.pad(early[None], ((0, 0), (0, padded - pairs)), constant_values=-1)
    late_all = jnp.pad(late[None], ((0, 0), (0, padded - pairs)), constant_values=-1)
    slots = (2 * LEVELS + 1) * SPAN * SPAN
    extra = keep_all.shape[0] - classes
    gap_all = jnp.pad(gap_dates, ((0, extra), (0, 0)), constant_values=-1)
    coef, near = pl.pallas_call(
        reduction_kernel,
        out_shape=[
            jax.ShapeDtypeStruct((slots, keep_all.shape[0], LANES), jnp.float32),
            jax.ShapeDtypeStruct((4, keep_all.shape[0], WIDE), jnp.float32),
        ],
        compiler_params=pltpu.CompilerParams(vmem_limit_bytes=48 << 20),
        cost_estimate=pl.CostEstimate(flops=1 << 32, bytes_accessed=1 << 20, transcendentals=0),
    )(keep_all, early_all, late_all, gap_all)
    coef = jnp.transpose(coef[:, :classes, :BLOCKS_PAD], (1, 2, 0))
    mix = mixing_matrix(near[:, :classes, :DATES_PAD])
    count = pairs // own[1]
    begin = own[0] * count
    cut = lambda value, fill: jnp.pad(
        lax.dynamic_slice_in_dim(value, begin, count, 1),
        ((0, 0), (0, width - count)),
        constant_values=fill,
    )
    line = pl.BlockSpec((1, width), lambda q: (0, 0))
    return pl.pallas_call(
        inverse_kernel,
        grid=(classes,),
        in_specs=[
            pl.BlockSpec((1, BLOCKS_PAD, slots), lambda q: (q, 0, 0)),
            pl.BlockSpec((1, DATES_PAD, SPAN * BLOCKS_PAD), lambda q: (q, 0, 0)),
            line,
            line,
            pl.BlockSpec((1, 1, width), lambda q: (q, 0, 0)),
        ],
        out_specs=pl.BlockSpec((1, DATES_PAD, width), lambda q: (q, 0, 0)),
        out_shape=jax.ShapeDtypeStruct((classes, DATES_PAD, width), jnp.bfloat16),
        scratch_shapes=[
            pltpu.VMEM((2, SPAN, BLOCKS_PAD + 2 * RIM, WIDE), jnp.float32),
            pltpu.VMEM((SPAN * BLOCKS_PAD, WIDE), jnp.float32),
        ],
        compiler_params=pltpu.CompilerParams(vmem_limit_bytes=48 << 20),
        cost_estimate=pl.CostEstimate(flops=3 << 33, bytes_accessed=4 << 20, transcendentals=0),
    )(coef, mix, cut(early[None], -1), cut(late[None], -1), cut(keep, 0.0)[:, None, :])


def edge_rows(value, axis, width, order=None):
    count, length = lax.axis_size(axis), value.shape[0] if order is None else value.shape[2]
    dim = 0 if order is None else 2
    up = [(i, (i + 1) % count) for i in range(count - 1)]
    down = [(j, i) for i, j in up]
    last = lax.slice_in_dim(value, length - width, length, axis=dim)
    leading = lax.slice_in_dim(value, 0, width, axis=dim)
    if order is not None:
        last, leading = jnp.transpose(last, order), jnp.transpose(leading, order)
    return lax.ppermute(last, axis, up), lax.ppermute(leading, axis, down)


def from_box(boxed, valid):
    power = boxed[0] * boxed[0] + boxed[1] * boxed[1]
    looks = boxed[1] * lax.rsqrt(jnp.maximum(power, 1.0))
    return jnp.where(valid, looks, 0.0).astype(jnp.bfloat16)


def within(pairs, batch, lanes):
    spot = lax.broadcasted_iota(jnp.int32, (batch, lanes), 0) + pl.program_id(0) * batch
    return spot < pairs


def inner_kernel(pairs, planes_ref, band_ref, out_ref, rim_ref, box_ref):
    batch, strip, columns = planes_ref.shape[1:]
    halves = columns // LANES
    for c in range(2):
        along = jnp.dot(
            planes_ref[c].reshape(batch * strip, columns),
            band_ref[...],
            preferred_element_type=jnp.float32,
        )
        for h in range(halves):
            box_ref[c, h] = along[:, h * LANES : (h + 1) * LANES]
    valid = within(pairs, batch, LANES)
    for h in range(halves):
        lanes = slice(h * LANES, (h + 1) * LANES)
        lines = [
            [box_ref[c, h, pl.ds(r, batch, stride=strip), :] for r in range(4)] for c in range(2)
        ]
        for c in range(2):
            near = (lines[c][0] + lines[c][1]) + lines[c][2]
            rim_ref[c, 0, :, lanes] = near
            rim_ref[c, 1, :, lanes] = near + lines[c][3]
        for r in range(2, strip - 2):
            boxed = []
            for c in range(2):
                lines[c].append(box_ref[c, h, pl.ds(r + 2, batch, stride=strip), :])
                a, b, d, e, f = lines[c]
                boxed.append((a + b) + (d + e) + f)
                lines[c].pop(0)
            out_ref[r - 2, :, lanes] = from_box(boxed, valid)
        for c in range(2):
            near = (lines[c][1] + lines[c][2]) + lines[c][3]
            rim_ref[c, 2, :, lanes] = near + lines[c][0]
            rim_ref[c, 3, :, lanes] = near


def outer_kernel(pairs, rim_ref, top_ref, bottom_ref, band_ref, out_ref):
    batch, columns = rim_ref.shape[2:]
    band = band_ref[...]
    valid = within(pairs, batch, columns)
    sums = []
    for c in range(2):
        above = [
            jnp.dot(top_ref[c, i], band, preferred_element_type=jnp.float32) for i in range(2)
        ]
        below = [
            jnp.dot(bottom_ref[c, i], band, preferred_element_type=jnp.float32) for i in range(2)
        ]
        sums.append(
            [
                rim_ref[c, 0] + (above[0] + above[1]),
                rim_ref[c, 1] + above[1],
                rim_ref[c, 2] + below[0],
                rim_ref[c, 3] + (below[0] + below[1]),
            ]
        )
    for r in range(4):
        out_ref[r] = from_box([sums[0][r], sums[1][r]], valid)


def pick_batch(width):
    return 96 if width % 96 == 0 else LANES


def column_band(columns):
    spots = np.arange(columns)
    return jnp.asarray(
        (np.abs(spots[:, None] - spots[None, :]) <= 2).astype(ml_dtypes.bfloat16)
    )


def multilook_inner(interferograms, width):
    pairs, strip, columns = interferograms.shape[1:]
    batch = pick_batch(width)
    return pl.pallas_call(
        functools.partial(inner_kernel, pairs),
        grid=(width // batch,),
        in_specs=[
            pl.BlockSpec((2, batch, strip, columns), lambda j: (0, j, 0, 0)),
            pl.BlockSpec((columns, columns), lambda j: (0, 0)),
        ],
        out_specs=[
            pl.BlockSpec((strip - 4, batch, columns), lambda j: (0, j, 0)),
            pl.BlockSpec((2, 4, batch, columns), lambda j: (0, 0, j, 0)),
        ],
        out_shape=[
            jax.ShapeDtypeStruct((strip - 4, width, columns), jnp.bfloat16),
            jax.ShapeDtypeStruct((2, 4, width, columns), jnp.float32),
        ],
        scratch_shapes=[
            pltpu.VMEM((2, columns // LANES, batch * strip, LANES), jnp.float32)
        ],
        compiler_params=pltpu.CompilerParams(vmem_limit_bytes=40 << 20),
        cost_estimate=pl.CostEstimate(flops=3 << 33, bytes_accessed=24 << 20, transcendentals=0),
    )(interferograms, column_band(columns))


def multilook_outer(rims, top, bottom, pairs):
    width, columns = rims.shape[2:]
    batch = pick_batch(width)
    edge = pl.BlockSpec((2, 2, batch, columns), lambda j: (0, 0, j, 0))
    return pl.pallas_call(
        functools.partial(outer_kernel, pairs),
        grid=(width // batch,),
        in_specs=[
            pl.BlockSpec((2, 4, batch, columns), lambda j: (0, 0, j, 0)),
            edge,
            edge,
            pl.BlockSpec((columns, columns), lambda j: (0, 0)),
        ],
        out_specs=pl.BlockSpec((4, batch, columns), lambda j: (0, j, 0)),
        out_shape=jax.ShapeDtypeStruct((4, width, columns), jnp.bfloat16),
        compiler_params=pltpu.CompilerParams(vmem_limit_bytes=40 << 20),
    )(rims, top, bottom, column_band(columns))


def series_kernel(half_ref, operator_ref, looks_ref, class_ref, out_ref):
    total = jnp.zeros((operator_ref.shape[1], looks_ref.shape[2]), jnp.float32)
    for q in range(operator_ref.shape[0]):
        solved = jnp.dot(operator_ref[q], looks_ref[0], preferred_element_type=jnp.float32)
        total = jnp.where(class_ref[0] == q, solved, total)
    out_ref[0] = total


def invert(operators, looks, pattern_ids, half, rows):
    classes, dates, width = operators.shape
    columns = looks.shape[2]
    return pl.pallas_call(
        series_kernel,
        grid_spec=pltpu.PrefetchScalarGridSpec(
            num_scalar_prefetch=1,
            grid=(rows,),
            in_specs=[
                pl.BlockSpec((classes, dates, width), lambda r, h: (0, 0, 0)),
                pl.BlockSpec((1, width, columns), lambda r, h: (h[0] * rows + r, 0, 0)),
                pl.BlockSpec((1, 1, columns), lambda r, h: (h[0] * rows + r, 0, 0)),
            ],
            out_specs=pl.BlockSpec((1, dates, columns), lambda r, h: (r, 0, 0)),
        ),
        out_shape=jax.ShapeDtypeStruct((rows, dates, columns), jnp.float32),
        compiler_params=pltpu.CompilerParams(vmem_limit_bytes=48 << 20),
        cost_estimate=pl.CostEstimate(
            flops=2 * classes * dates * width * columns * rows,
            bytes_accessed=2 * rows * width * columns + 4 * rows * dates * columns,
            transcendentals=0,
        ),
    )(jnp.reshape(half, (1,)), operators, looks, pattern_ids[:, None, :])


def gauss_taps():
    spots = np.arange(-RADIUS, RADIUS + 1)
    raw = np.exp(-spots * spots / (2.0 * gauss_width * gauss_width))
    return raw / raw.sum()


def screen_kernel(taps, series_ref, before_ref, after_ref, high_ref, low_ref, out_ref):
    rows, tile, columns = series_ref.shape
    lines = [before_ref[i].astype(jnp.float32) for i in range(RADIUS)]
    lines += [series_ref[i] for i in range(rows)]
    lines += [after_ref[i].astype(jnp.float32) for i in range(RADIUS)]
    for r in range(rows):
        total = taps[RADIUS] * lines[r + RADIUS]
        for a in range(RADIUS):
            total += taps[a] * (lines[r + a] + lines[r + 2 * RADIUS - a])
        high = total.astype(jnp.bfloat16)
        low = (total - high.astype(jnp.float32)).astype(jnp.bfloat16)
        screen = jnp.dot(low, high_ref[...], preferred_element_type=jnp.float32)
        screen += jnp.dot(high, low_ref[...], preferred_element_type=jnp.float32)
        screen += jnp.dot(high, high_ref[...], preferred_element_type=jnp.float32)
        out_ref[:, r, :] = series_ref[r] - screen


def remove_screen(series, before, after):
    rows, dates, columns = series.shape
    taps = gauss_taps()
    spots = np.arange(columns)
    lag = spots[:, None] - spots[None, :]
    band = np.where(np.abs(lag) <= RADIUS, taps[np.clip(lag, -RADIUS, RADIUS) + RADIUS], 0.0)
    band = band.astype(np.float32)
    high = band.astype(ml_dtypes.bfloat16)
    low = (band - high.astype(np.float32)).astype(ml_dtypes.bfloat16)
    tile = 64
    piece = lambda count: pl.BlockSpec((count, tile, columns), lambda t: (0, t, 0))
    square = pl.BlockSpec((columns, columns), lambda t: (0, 0))
    corrected = pl.pallas_call(
        functools.partial(screen_kernel, [float(x) for x in taps]),
        grid=(-(-dates // tile),),
        in_specs=[piece(rows), piece(RADIUS), piece(RADIUS), square, square],
        out_specs=pl.BlockSpec((tile, rows, columns), lambda t: (t, 0, 0)),
        out_shape=jax.ShapeDtypeStruct((DATES, rows, columns), jnp.float32),
        compiler_params=pltpu.CompilerParams(vmem_limit_bytes=48 << 20),
    )(series, before, after, jnp.asarray(high), jnp.asarray(low))
    return jnp.transpose(corrected, (1, 0, 2))


def body(interferograms, pair_dates, mask_table, gap_dates, pattern_ids):
    pairs, strip = interferograms.shape[1:3]
    shares = lax.axis_size("pairs")
    place = lax.axis_index("pairs")
    width = round_up(pairs, LANES)
    top, bottom = edge_rows(interferograms, "rows", 2, (0, 2, 1, 3))
    operators = build_operators(pair_dates, mask_table, gap_dates, (place, shares), width)
    inner_looks, rims = multilook_inner(interferograms, width)
    inner_ids = pattern_ids[2 : strip - 2]
    outer_ids = jnp.concatenate([pattern_ids[:2], pattern_ids[strip - 2 :]])
    across = [(i, 1 - i) for i in range(shares)]
    inner_away = invert(operators, inner_looks, inner_ids, 1 - place, strip // 2 - 2)
    inner_got = lax.ppermute(inner_away, "pairs", across)
    inner_own = invert(operators, inner_looks, inner_ids, place, strip // 2 - 2)
    rims, inner_own = lax.optimization_barrier((rims, inner_own))
    outer_looks = multilook_outer(rims, top, bottom, pairs)
    outer_away = invert(operators, outer_looks, outer_ids, 1 - place, 2)
    outer_got = lax.ppermute(outer_away, "pairs", across)
    outer_own = invert(operators, outer_looks, outer_ids, place, 2)
    inner = inner_own + inner_got
    outer = outer_own + outer_got
    series = jnp.where(
        place == 0,
        jnp.concatenate([outer, inner]),
        jnp.concatenate([inner, outer]),
    )
    before, after = edge_rows_bf16(series)
    return remove_screen(series, before, after)


def edge_rows_bf16(series):
    return edge_rows(series.astype(jnp.bfloat16), ("rows", "pairs"), RADIUS)


def solution(mesh):
    placed = (
        P(None, "pairs", ("blocks", "rows"), None),
        P(),
        P(),
        P(),
        P(("blocks", "rows"), None),
    )
    return jax.shard_map(
        body,
        mesh=mesh,
        in_specs=placed,
        out_specs=P(("blocks", "rows", "pairs"), None, None),
        check_vma=False,
    )
```
